128 devices in a mesh: rows: 16 (over y, z), cols: 4 (over x_lo, core), dp: 2 (over x_hi).
Axes of the slice: x: 4 (x_hi: 2, x_lo: 2; x = x_hi * 2 + x_lo), y: 4, z: 4, core: 2. Of those that a mesh axis runs over, the one named last changes fastest.
Arguments:
- panel_weight: float32 [8192, 1024], P('rows', 'cols'), may hold values from -6 to 6
- rest_weight: float32 [8192, 15360], P('rows', 'cols'), may hold values from -6 to 6
- hinv_diag: float32 [1024, 1024], P('rows'), as said below
- hinv_off: float32 [1024, 15360], P('rows', 'cols'), may hold values from -0.1875 to 0.1875
- calib_panel: bfloat16 [1024, 1024], P('dp', 'cols'), may hold values from -0.125 to 0.125
- calib_rest: bfloat16 [1024, 15360], P('dp', 'cols'), may hold values from -0.125 to 0.125
- prune_blocks: int32 [128, 8], P('rows'), may hold values from 0 to 15, as said below
Outputs:
- pruned_panel: float32 [8192, 1024], P('rows', 'cols')
- pruned_rest: float32 [8192, 15360], P('rows', 'cols')
- layer_out: bfloat16 [1024, 8192], P('dp', ('rows', 'cols'))
- recon_error: float32 [1024, 8192], P('dp', ('rows', 'cols'))
The draws below stay inside these ranges and needn't reach their ends.
Inputs may be any that keep to these rules, and one draw needn't show every extreme that they name: `prune_blocks`: each row names 8 different column blocks of the panel's 16. `hinv_diag`: upper triangular with a positive diagonal.
All inputs are finite; a program needn't handle non-finite values.
Results may differ from the reference program's by a relative error of at most 0.0098.
Values sent between devices are 32-bit elements; how exact they have to be, the bound alone decides.
No kernel may reach another device: no remote copies, remote signals or barrier semaphores. Data moves between devices by JAX's collectives and lax.ppermute only.
A program may use at most 128 MiB of HBM per device.

```python
import jax
import jax.numpy as jnp
from jax import lax

D = 16384
PC = 1024
BLOCK = 64
KP = 8
BLOCKS = 16
REST = 15360
OUT_ROWS = 8192
TOKENS = 1024


def draw_hinv_diag(key, part):
    key = jax.random.fold_in(key, 11)
    first, second = jax.random.split(key)
    spread = 0.6 / PC ** 0.5
    rough = jax.random.normal(first, (PC, PC), jnp.float32) * spread
    diag = jnp.exp(jax.random.uniform(second, (PC,), jnp.float32, 0.0, 1.0986123))
    upper = jnp.triu(rough, 1)
    return upper + jnp.diag(diag)


def draw_prune_blocks(key, part):
    key = jax.random.fold_in(key, 23)
    keys = jax.random.split(key, OUT_ROWS // BLOCK)
    chosen = jax.vmap(lambda k: jax.random.permutation(k, BLOCKS)[:KP])(keys)
    return chosen.astype(jnp.int32)


def shard_levels(stream_key, dims, cuts, least, top_value):
    def one(axis_at, parts):
        steps = jax.random.uniform(jax.random.fold_in(jax.random.fold_in(stream_key, 6), axis_at), (parts,), jnp.float32, least / len(cuts), top_value / len(cuts))
        return jnp.repeat(jnp.exp(steps), dims[axis_at] // parts).reshape((-1,) + (1,) * (len(dims) - axis_at - 1))

    factor_of = one(*cuts[0])
    for cut in cuts[1:]:
        factor_of = factor_of * one(*cut)
    return factor_of


def gaussian(stream_key, shape, deviation, reach, shards=(), held_as=jnp.bfloat16):
    gain = shard_levels(stream_key, shape, shards, -0.22, 0.18) if shards else 1.0
    array = jax.random.normal(stream_key, shape, jnp.float32) * deviation * gain
    return jnp.minimum(jnp.maximum(array, -reach), reach).astype(held_as)


def setup_inputs(seed: int = 0) -> dict:
    key_of = jax.random.split(jax.random.key(seed), 8)
    panel_weight = gaussian(key_of[0], (OUT_ROWS, PC), 1.0, 6.0, ((0, 16), (1, 4)), jnp.float32)
    rest_weight = gaussian(key_of[1], (OUT_ROWS, REST), 1.0, 6.0, ((0, 16), (1, 4)), jnp.float32)
    hinv_diag = draw_hinv_diag(jax.random.fold_in(key_of[7], 71), 0)
    hinv_off = gaussian(key_of[3], (PC, REST), PC ** -0.5, 0.1875, ((0, 16), (1, 4)), jnp.float32)
    calib_panel = gaussian(key_of[4], (TOKENS, PC), (D ** -0.5), 0.125, ((0, 2), (1, 4)))
    calib_rest = gaussian(key_of[5], (TOKENS, REST), (D ** -0.5), 0.125, ((0, 2), (1, 4)))
    prune_blocks = draw_prune_blocks(jax.random.fold_in(key_of[7], 71), 0)
    return dict(panel_weight=panel_weight, rest_weight=rest_weight, hinv_diag=hinv_diag, hinv_off=hinv_off, calib_panel=calib_panel, calib_rest=calib_rest, prune_blocks=prune_blocks)


def block_mask(prune_blocks):
    hits = prune_blocks[:, :, None] == jnp.arange(BLOCKS, dtype=jnp.int32)[None, None, :]
    dense = jnp.sum(hits.astype(jnp.float32), axis=1)
    dense = jnp.repeat(jnp.repeat(dense, BLOCK, axis=0), BLOCK, axis=1)
    return dense

def project(inputs, weights):
    return jnp.einsum('tk,rk->tr', inputs.astype(jnp.float32), weights.astype(jnp.float32), preferred_element_type=jnp.float32)

def reference(panel_weight, rest_weight, hinv_diag, hinv_off, calib_panel, calib_rest, prune_blocks):
    mask = block_mask(prune_blocks)
    work = panel_weight
    pieces = []
    for block in range(BLOCKS):
        lower_edge = block * BLOCK
        upper_edge = lower_edge + BLOCK
        target = work[:, lower_edge:upper_edge] * mask[:, lower_edge:upper_edge]
        square = hinv_diag[lower_edge:upper_edge, lower_edge:upper_edge]
        err = jax.scipy.linalg.solve_triangular(square, target.T, trans=1, lower=False).T
        work = work - jnp.dot(err, hinv_diag[lower_edge:upper_edge, :], precision=lax.Precision.HIGHEST)
        pieces.append(err)
    errors = jnp.concatenate(pieces, axis=1)
    pruned_panel = work * (1.0 - mask)
    pruned_rest = rest_weight - jnp.dot(errors, hinv_off, precision=lax.Precision.HIGHEST)
    pruned_sum = project(calib_panel, pruned_panel.astype(jnp.bfloat16)) + project(calib_rest, pruned_rest.astype(jnp.bfloat16))
    dense_sum = project(calib_panel, panel_weight.astype(jnp.bfloat16)) + project(calib_rest, rest_weight.astype(jnp.bfloat16))
    return (pruned_panel, pruned_rest, pruned_sum.astype(jnp.bfloat16), pruned_sum - dense_sum)
```

```python
import functools

import jax
import jax.numpy as jnp
from jax import lax
from jax.experimental import pallas as pl
from jax.experimental.pallas import tpu as pltpu
from jax.sharding import PartitionSpec as P

BLOCK = 64
RING = 4
OFFSETS = (0, -1, 1, 2)
F32 = jnp.float32
BF16 = jnp.bfloat16
HIGHEST = lax.Precision.HIGHEST


def split(value):
    high = value.astype(BF16)
    low = (value - high.astype(F32)).astype(BF16)
    return high, low


def dot(left, right):
    return jnp.dot(left, right, preferred_element_type=F32)


def dot3(left, right):
    return dot(left[0], right[0]) + dot(left[1], right[0]) + dot(left[0], right[1])


def dot_nt(left, right):
    return lax.dot_general(left, right, (((1,), (1,)), ((), ())), preferred_element_type=F32)


def along(value, axis, step):
    def shift(y, z):
        if axis == "y":
            return ((y + step) % RING) * RING + z
        return y * RING + (z + step) % RING

    pairs = [(y * RING + z, shift(y, z)) for y in range(RING) for z in range(RING)]
    return lax.ppermute(value, "rows", pairs)


def swap(value, bit):
    return lax.ppermute(value, "cols", [(i, i ^ bit) for i in range(4)])


def ring_gather(value, axis):
    half = value.shape[0] // 2
    before, after = along(value, axis, 1), along(value, axis, -1)
    far_top, far_bottom = along(before[:half], axis, 1), along(after[half:], axis, -1)
    return jnp.concatenate([value, before, after, far_top, far_bottom], axis=0)


def factor_kernel(place, diag_ref, rows_ref, out_ref):
    block, core = place[0], place[1]
    side = BLOCK
    row = lax.broadcasted_iota(jnp.int32, (side, side), 0)
    column = lax.broadcasted_iota(jnp.int32, (side, side), 1)
    square = diag_ref[...]
    identity = (row == column).astype(F32)
    down = jnp.sum(square * identity, axis=1, keepdims=True)
    across = jnp.sum(square * identity, axis=0, keepdims=True)
    power = jnp.where(column > row, -(square / down), 0.0)
    inverse = identity + power
    for _ in range(side.bit_length() - 2):
        power = jnp.dot(power, power, precision=HIGHEST, preferred_element_type=F32)
        inverse = jnp.dot(inverse, identity + power, precision=HIGHEST, preferred_element_type=F32)
    inverse = inverse / across
    width = out_ref.shape[1]
    start = pl.multiple_of(core * width, width)
    mine = rows_ref[:, pl.ds(start, width)]
    local = lax.broadcasted_iota(jnp.int32, (side, width), 1) + start - block * side
    wide_row = lax.broadcasted_iota(jnp.int32, (side, width), 0)
    inside = (local >= 0) & (local < side)
    mine = jnp.where(inside, (local == wide_row).astype(F32), mine)
    out_ref[...] = jnp.dot(inverse, mine, precision=HIGHEST, preferred_element_type=F32)


def chain_kernel(
    place, prune_ref, w0, w1, w2, w3, near_ref, far_ref,
    high_ref, low_ref, kept_ref,
    work, fac_high, fac_low, kept,
):
    col, core, y, z = place[2], place[1], place[3], place[4]
    rows, own = w0.shape
    for slot, piece in enumerate((w0, w1, w2, w3)):
        work[col ^ slot] = piece[...]
    half = near_ref.shape[1]
    for which, ref in enumerate((near_ref, far_ref)):
        start = pl.multiple_of((core ^ which) * half, half)
        for zi, zo in enumerate(OFFSETS):
            for yi, yo in enumerate(OFFSETS):
                block = ((y + yo) & 3) * RING + ((z + zo) & 3)
                at = (zi * RING + yi) * BLOCK
                top = pl.multiple_of(block * BLOCK, BLOCK)
                high, low = split(ref[at : at + BLOCK, :])
                fac_high[pl.ds(top, BLOCK), pl.ds(start, half)] = high
                fac_low[pl.ds(top, BLOCK), pl.ds(start, half)] = low
    groups = rows // BLOCK
    bits = []
    for group in range(groups):
        word = jnp.int32(0)
        for entry in range(prune_ref.shape[1]):
            word = word | (jnp.int32(1) << prune_ref[group, entry])
        bits.append(jnp.full((BLOCK, 128), word, jnp.int32))
    lane = lax.broadcasted_iota(jnp.int32, (rows, 128), 1)
    upper = lane >> 6
    bits = lax.shift_right_logical(jnp.concatenate(bits, axis=0), upper)
    lower = 1 - upper
    panels = work.shape[0]
    parts = 2
    size = rows // parts
    for panel in range(panels):
        base = panel * own
        for part in range(parts):
            rs = slice(part * size, (part + 1) * size)
            word, first_half = bits[rs], lower[rs]
            left = work[panel, rs, :128]
            right = work[panel, rs, 128:]
            targets = []
            pair_values = [left, right]
            for pair in range(2):
                value = pair_values[pair]
                first = panel * 4 + pair * 2
                top = base + pair * 128
                hit = lax.shift_right_logical(word, first) & 1
                t0 = jnp.where((hit & first_half) != 0, value, 0.0)
                fac = (
                    fac_high[top : top + 128, top : top + 128],
                    fac_low[top : top + 128, top : top + 128],
                )
                step = dot3(split(t0), fac)
                value = jnp.where(first_half != 0, value, value - step)
                target = jnp.where(hit != 0, value, 0.0)
                keep = jnp.where(hit != 0, 0.0, value)
                kept[panel, rs, pair * 128 : (pair + 1) * 128] = keep
                targets.append(target)
                if pair == 0:
                    fac = (
                        fac_high[top : top + 128, top + 128 : top + 256],
                        fac_low[top : top + 128, top + 128 : top + 256],
                    )
                    pair_values[1] = right - dot3(split(target), fac)
            target = split(jnp.concatenate(targets, axis=1))
            r = lax.broadcasted_iota(jnp.int32, (own, own), 0)
            c = lax.broadcasted_iota(jnp.int32, (own, own), 1)
            same = (r // BLOCK) == (c // BLOCK)
            zero = jnp.zeros((own, own), BF16)
            diagonal = (
                jnp.where(same, fac_high[base : base + own, base : base + own], zero),
                jnp.where(same, fac_low[base : base + own, base : base + own], zero),
            )
            errors = split(dot3(target, diagonal))
            high_ref[rs, base : base + own] = errors[0]
            low_ref[rs, base : base + own] = errors[1]
            for later in range(panel + 1, panels):
                to = later * own
                fac = (
                    fac_high[base : base + own, to : to + own],
                    fac_low[base : base + own, to : to + own],
                )
                work[later, rs, :] = work[later, rs, :] - dot3(target, fac)
    kept_ref[...] = kept[col]


def store_slots(place, total, keep_ref, send_ref):
    col = place[2]
    width = keep_ref.shape[2]
    for slot in range(4):
        ref = send_ref if slot & 1 else keep_ref
        group = col ^ slot
        for source in range(4):

            @pl.when(group == source)
            def _():
                ref[slot >> 1] = total[:, source * width : (source + 1) * width]


def forward_kernel(place, panel_ref, calib_panel_ref, rest_ref, calib_ref, keep_ref, send_ref, total):
    step = pl.program_id(0)

    @pl.when(step == 0)
    def _():
        total[...] = dot_nt(calib_panel_ref[...], panel_ref[...].astype(BF16))

    total[...] += dot_nt(calib_ref[...], rest_ref[...].astype(BF16))

    @pl.when(step == pl.num_programs(0) - 1)
    def _():
        store_slots(place, total, keep_ref, send_ref)


def update_kernel(
    place, panel_ref, calib_panel_ref, high_ref, low_ref, rest_ref, factor_ref, calib_ref,
    new_ref, keep_ref, send_ref, total,
):
    step = pl.program_id(0)

    @pl.when(step == 0)
    def _():
        total[...] = dot_nt(calib_panel_ref[...], panel_ref[...].astype(BF16))

    value = rest_ref[...] - dot3((high_ref[...], low_ref[...]), split(factor_ref[...]))
    new_ref[...] = value
    total[...] += dot_nt(calib_ref[...], value.astype(BF16))

    @pl.when(step == pl.num_programs(0) - 1)
    def _():
        store_slots(place, total, keep_ref, send_ref)


SMEM = pl.BlockSpec(memory_space=pltpu.SMEM)
VMEM = pl.BlockSpec(memory_space=pltpu.VMEM)


def params(mib, **more):
    return pltpu.CompilerParams(vmem_limit_bytes=mib * 2**20, **more)


def cost(flops, moved):
    return pl.CostEstimate(flops=flops, bytes_accessed=moved, transcendentals=0)


def slots(rows, tokens):
    shape = jax.ShapeDtypeStruct((2, tokens, rows // 4), F32)
    spec = pl.BlockSpec((2, tokens, rows // 4), lambda i: (0, 0, 0))
    return [shape, shape], [spec, spec]


def whole(shape):
    return pl.BlockSpec(shape, lambda i: (0,) * len(shape))


def tiles(rows, width):
    return pl.BlockSpec((rows, width), lambda i: (0, i))


def forward(place, panel, calib_panel, rest, calib):
    rows, columns = rest.shape
    tokens = calib.shape[0]
    tile = 384
    shapes, specs = slots(rows, tokens)
    return pl.pallas_call(
        forward_kernel,
        grid=(columns // tile,),
        in_specs=[
            SMEM, whole(panel.shape), whole(calib_panel.shape),
            tiles(rows, tile), tiles(tokens, tile),
        ],
        out_specs=specs,
        out_shape=shapes,
        scratch_shapes=[pltpu.VMEM((tokens, rows), F32)],
        compiler_params=params(32),
        cost_estimate=cost(2 * rows * tokens * columns, rows * columns * 4 + tokens * columns * 2),
    )(place, panel, calib_panel, rest, calib)


def update(place, panel, calib_panel, high, low, rest, factor, calib):
    rows, columns = rest.shape
    tokens = calib.shape[0]
    depth = factor.shape[0]
    tile = 384
    shapes, specs = slots(rows, tokens)
    return pl.pallas_call(
        update_kernel,
        grid=(columns // tile,),
        in_specs=[
            SMEM, whole(panel.shape), whole(calib_panel.shape), whole(high.shape), whole(low.shape),
            tiles(rows, tile), tiles(depth, tile), tiles(tokens, tile),
        ],
        out_specs=[tiles(rows, tile)] + specs,
        out_shape=[jax.ShapeDtypeStruct(rest.shape, F32)] + shapes,
        scratch_shapes=[pltpu.VMEM((tokens, rows), F32)],
        compiler_params=params(40),
        cost_estimate=cost(
            2 * rows * columns * (3 * depth + tokens), columns * 4 * (2 * rows + depth)
        ),
    )(place, panel, calib_panel, high, low, rest, factor, calib)


def scatter_sum(keep, send):
    near = keep + swap(send, 1)
    return near[0] + swap(near[1], 2)


def on_device(
    panel_weight, rest_weight, hinv_diag, hinv_off, calib_panel, calib_rest, prune_blocks
):
    col = lax.axis_index("cols")
    block = lax.axis_index("rows")
    core = col % 2
    place = jnp.stack([block, core, col, block // RING, block % RING]).astype(jnp.int32)
    rows, own = panel_weight.shape
    panel = hinv_diag.shape[1]
    gathered = lax.all_gather(hinv_off, "rows", axis=0, tiled=True)

    square = lax.dynamic_slice(hinv_diag, (0, block * BLOCK), (BLOCK, BLOCK))
    mine = pl.pallas_call(
        factor_kernel,
        in_specs=[SMEM, VMEM, VMEM],
        out_specs=VMEM,
        out_shape=jax.ShapeDtypeStruct((BLOCK, panel // 2), F32),
        cost_estimate=cost(2 * 64 * 64 * 1600 * 6, 2 * 64 * 1024 * 4),
    )(place, square, hinv_diag)
    near = ring_gather(ring_gather(mine, "y"), "z")
    far = swap(near, 1)

    across = swap(panel_weight, 2)
    pieces = [panel_weight, swap(panel_weight, 1), across, swap(across, 1)]

    high, low, kept = pl.pallas_call(
        chain_kernel,
        in_specs=[SMEM, SMEM] + [VMEM] * 6,
        out_specs=[VMEM] * 3,
        out_shape=[
            jax.ShapeDtypeStruct((rows, panel), BF16),
            jax.ShapeDtypeStruct((rows, panel), BF16),
            jax.ShapeDtypeStruct((rows, own), F32),
        ],
        scratch_shapes=[
            pltpu.VMEM((4, rows, own), F32),
            pltpu.VMEM((panel, panel), BF16),
            pltpu.VMEM((panel, panel), BF16),
            pltpu.VMEM((4, rows, own), F32),
        ],
        compiler_params=params(40),
        cost_estimate=cost(2 * rows * panel * panel * 6, rows * panel * 8 + panel * panel * 4),
    )(place, prune_blocks, *pieces, near, far)

    dense = scatter_sum(*forward(place, panel_weight, calib_panel, rest_weight, calib_rest))
    new_rest, keep, send = update(
        place, kept, calib_panel, high, low, rest_weight, gathered, calib_rest
    )
    pruned = scatter_sum(keep, send)
    return kept, new_rest, pruned.astype(BF16), pruned - dense


def solution(mesh):
    in_specs = (
        P("rows", "cols"),
        P("rows", "cols"),
        P("rows", None),
        P("rows", "cols"),
        P("dp", "cols"),
        P("dp", "cols"),
        P("rows", None),
    )
    out_specs = (
        P("rows", "cols"),
        P("rows", "cols"),
        P("dp", ("rows", "cols")),
        P("dp", ("rows", "cols")),
    )
    return jax.shard_map(
        on_device, mesh=mesh, in_specs=in_specs, out_specs=out_specs, check_vma=False
    )
```

```python
import functools

import jax
import jax.numpy as jnp
from jax import lax
from jax.experimental import pallas as pl
from jax.experimental.pallas import tpu as pltpu
from jax.sharding import PartitionSpec as P

BLOCK = 64
UPDATE_MIB = 56
RING = 4
OFFSETS = (0, -1, 1, 2)
GROUP = 256
TILE = 768
F32 = jnp.float32
BF16 = jnp.bfloat16
HIGHEST = lax.Precision.HIGHEST


def split(value):
    high = value.astype(BF16)
    low = (value - high.astype(F32)).astype(BF16)
    return high, low


def dot(left, right):
    return jnp.dot(left, right, preferred_element_type=F32)


def dot3(left, right):
    return dot(left[0], right[0]) + dot(left[1], right[0]) + dot(left[0], right[1])


def dot_nt(left, right):
    return lax.dot_general(left, right, (((1,), (1,)), ((), ())), preferred_element_type=F32)


def along(value, axis, step):
    if axis == "x":
        pairs = []
        for x in range(RING):
            to = (x + step) % RING
            for core in range(2):
                pairs.append((((x % 2) * 2 + core) * 2 + x // 2, ((to % 2) * 2 + core) * 2 + to // 2))
        return lax.ppermute(value, ("cols", "dp"), pairs)

    def shift(y, z):
        if axis == "y":
            return ((y + step) % RING) * RING + z
        return y * RING + (z + step) % RING

    pairs = [(y * RING + z, shift(y, z)) for y in range(RING) for z in range(RING)]
    return lax.ppermute(value, "rows", pairs)


def swap(value, bit):
    return lax.ppermute(value, "cols", [(i, i ^ bit) for i in range(4)])


def both_ways(value, axis):
    return along(value, axis, 1), along(value, axis, -1)


def halves(pair):
    before, after = pair
    half = before.shape[0] // 2
    return before[:half], after[half:]


def onward(pair, axis):
    top, bottom = pair
    return along(top, axis, 1), along(bottom, axis, -1)


def after(value, *others):
    return lax.optimization_barrier((value, others))[0]


def rows_of(value):
    return value.reshape(-1, value.shape[-1])


def factor_kernel(place, rows_ref, out_ref):
    block, core = place[0], place[1]
    side = BLOCK
    row = lax.broadcasted_iota(jnp.int32, (side, side), 0)
    column = lax.broadcasted_iota(jnp.int32, (side, side), 1)
    pair = rows_ref[:, pl.ds(pl.multiple_of((block >> 1) * 128, 128), 128)]
    square = jnp.where((block & 1) != 0, pair[:, side:], pair[:, :side])
    identity = (row == column).astype(F32)
    down = jnp.sum(square * identity, axis=1, keepdims=True)
    across = jnp.sum(square * identity, axis=0, keepdims=True)
    power = jnp.where(column > row, -(square / down), 0.0)
    inverse = identity + power
    for _ in range(side.bit_length() - 2):
        power = jnp.dot(power, power, precision=HIGHEST, preferred_element_type=F32)
        inverse = jnp.dot(inverse, identity + power, precision=HIGHEST, preferred_element_type=F32)
    inverse = inverse / across
    width = out_ref.shape[1]
    start = pl.multiple_of((place[5] * 2 + core) * width, width)
    mine = rows_ref[:, pl.ds(start, width)]
    local = lax.broadcasted_iota(jnp.int32, (side, width), 1) + start - block * side
    wide_row = lax.broadcasted_iota(jnp.int32, (side, width), 0)
    inside = (local >= 0) & (local < side)
    mine = jnp.where(inside, (local == wide_row).astype(F32), mine)
    out_ref[...] = jnp.dot(inverse, mine, precision=HIGHEST, preferred_element_type=F32)


def chain_kernel(
    place, prune_ref, w0, w1, w2, w3, near_ref, far_ref,
    high_ref, low_ref, kept_ref,
    work, fac_high, fac_low, kept,
):
    col, core, x = place[2], place[1], place[5]
    rows, own = w0.shape
    for slot, piece in enumerate((w0, w1, w2, w3)):
        work[col ^ slot] = piece[...]
    width = near_ref.shape[-1]
    for which, ref in enumerate((near_ref, far_ref)):
        for slot, offset in enumerate(OFFSETS):
            piece = ((x + offset) & 3) * 2 + (core ^ which)
            start = pl.multiple_of(piece * width, width)
            high, low = split(ref[slot])
            fac_high[:, pl.ds(start, width)] = high
            fac_low[:, pl.ds(start, width)] = low
    groups = rows // BLOCK
    bits = []
    for group in range(groups):
        word = jnp.int32(0)
        for entry in range(prune_ref.shape[1]):
            word = word | (jnp.int32(1) << prune_ref[group, entry])
        bits.append(jnp.full((BLOCK, 128), word, jnp.int32))
    lane = lax.broadcasted_iota(jnp.int32, (rows, 128), 1)
    upper = lane >> 6
    bits = lax.shift_right_logical(jnp.concatenate(bits, axis=0), upper)
    lower = 1 - upper
    panels = work.shape[0]
    parts = 2
    size = rows // parts
    for panel in range(panels):
        base = panel * own
        for part in range(parts):
            rs = slice(part * size, (part + 1) * size)
            word, first_half = bits[rs], lower[rs]
            left = work[panel, rs, :128]
            right = work[panel, rs, 128:]
            targets = []
            pair_values = [left, right]
            for pair in range(2):
                value = pair_values[pair]
                first = panel * 4 + pair * 2
                top = base + pair * 128
                hit = lax.shift_right_logical(word, first) & 1
                t0 = jnp.where((hit & first_half) != 0, value, 0.0)
                fac = (
                    fac_high[top : top + 128, top : top + 128],
                    fac_low[top : top + 128, top : top + 128],
                )
                step = dot3(split(t0), fac)
                value = jnp.where(first_half != 0, value, value - step)
                target = jnp.where(hit != 0, value, 0.0)
                keep = jnp.where(hit != 0, 0.0, value)
                kept[panel, rs, pair * 128 : (pair + 1) * 128] = keep
                targets.append(target)
                if pair == 0:
                    fac = (
                        fac_high[top : top + 128, top + 128 : top + 256],
                        fac_low[top : top + 128, top + 128 : top + 256],
                    )
                    pair_values[1] = right - dot3(split(target), fac)
            target = split(jnp.concatenate(targets, axis=1))
            r = lax.broadcasted_iota(jnp.int32, (own, own), 0)
            c = lax.broadcasted_iota(jnp.int32, (own, own), 1)
            same = (r // BLOCK) == (c // BLOCK)
            zero = jnp.zeros((own, own), BF16)
            diagonal = (
                jnp.where(same, fac_high[base : base + own, base : base + own], zero),
                jnp.where(same, fac_low[base : base + own, base : base + own], zero),
            )
            errors = split(dot3(target, diagonal))
            high_ref[rs, base : base + own] = errors[0]
            low_ref[rs, base : base + own] = errors[1]
            for later in range(panel + 1, panels):
                to = later * own
                fac = (
                    fac_high[base : base + own, to : to + own],
                    fac_low[base : base + own, to : to + own],
                )
                work[later, rs, :] = work[later, rs, :] - dot3(target, fac)
    kept_ref[...] = kept[col]


def store_slots(place, total, keep_ref, send_ref):
    col = place[2]
    width = keep_ref.shape[2]
    for slot in range(4):
        ref = send_ref if slot & 1 else keep_ref
        group = col ^ slot
        for source in range(4):

            @pl.when(group == source)
            def _():
                ref[slot >> 1] = total[:, source * width : (source + 1) * width]


def forward_kernel(place, panel_ref, calib_panel_ref, rest_ref, calib_ref, keep_ref, send_ref, total):
    step = pl.program_id(0)

    @pl.when(step == 0)
    def _():
        total[...] = dot_nt(calib_panel_ref[...], panel_ref[...].astype(BF16))

    total[...] += dot_nt(calib_ref[...], rest_ref[...].astype(BF16))

    @pl.when(step == pl.num_programs(0) - 1)
    def _():
        store_slots(place, total, keep_ref, send_ref)


def update_kernel(
    place, panel_ref, calib_panel_ref, high_ref, low_ref, rest_ref, factor_ref, calib_ref,
    new_ref, keep_ref, send_ref, total,
):
    step = pl.program_id(0)

    @pl.when(step == 0)
    def _():
        total[...] = dot_nt(calib_panel_ref[...], panel_ref[...].astype(BF16))

    value = rest_ref[...] - dot3((high_ref[...], low_ref[...]), split(factor_ref[...]))
    new_ref[...] = value
    total[...] += dot_nt(calib_ref[...], value.astype(BF16))

    @pl.when(step == pl.num_programs(0) - 1)
    def _():
        store_slots(place, total, keep_ref, send_ref)


SMEM = pl.BlockSpec(memory_space=pltpu.SMEM)
VMEM = pl.BlockSpec(memory_space=pltpu.VMEM)


def params(mib, **more):
    return pltpu.CompilerParams(vmem_limit_bytes=mib * 2**20, **more)


def cost(flops, moved):
    return pl.CostEstimate(flops=flops, bytes_accessed=moved, transcendentals=0)


def slots(rows, tokens):
    shape = jax.ShapeDtypeStruct((2, tokens, rows // 4), F32)
    spec = pl.BlockSpec((2, tokens, rows // 4), lambda i: (0, 0, 0))
    return [shape, shape], [spec, spec]


def whole(shape):
    return pl.BlockSpec(shape, lambda i: (0,) * len(shape))


def tiles(rows, width):
    return pl.BlockSpec((rows, width), lambda i: (0, i))


def forward(place, panel, calib_panel, rest, calib):
    rows, columns = rest.shape
    tokens = calib.shape[0]
    tile = 384
    shapes, specs = slots(rows, tokens)
    return pl.pallas_call(
        forward_kernel,
        grid=(columns // tile,),
        in_specs=[
            SMEM, whole(panel.shape), whole(calib_panel.shape),
            tiles(rows, tile), tiles(tokens, tile),
        ],
        out_specs=specs,
        out_shape=shapes,
        scratch_shapes=[pltpu.VMEM((tokens, rows), F32)],
        compiler_params=params(16),
        cost_estimate=cost(2 * rows * tokens * columns, rows * columns * 4 + tokens * columns * 2),
    )(place, panel, calib_panel, rest, calib)


def update(place, panel, calib_panel, errors, rest, factor, calib):
    rows, columns = rest.shape
    tokens = calib.shape[0]
    depth = factor.shape[0]
    shapes, specs = slots(rows, tokens)
    operands = (place, panel, calib_panel, *errors, rest, factor, calib)
    return pl.pallas_call(
        update_kernel,
        grid=(columns // TILE,),
        in_specs=[SMEM] + [whole(v.shape) for v in operands[1:5]]
        + [tiles(rows, TILE), tiles(depth, TILE), tiles(tokens, TILE)],
        out_specs=[tiles(rows, TILE)] + specs,
        out_shape=[jax.ShapeDtypeStruct(rest.shape, F32)] + shapes,
        scratch_shapes=[pltpu.VMEM((tokens, rows), F32)],
        compiler_params=params(UPDATE_MIB),
        cost_estimate=cost(
            2 * rows * columns * (3 * depth + tokens), columns * 4 * (2 * rows + depth)
        ),
    )(*operands)


def scatter_sum(keep, send):
    near = keep + swap(send, 1)
    return near[0] + swap(near[1], 2)


def on_device(
    panel_weight, rest_weight, hinv_diag, hinv_off, calib_panel, calib_rest, prune_blocks
):
    col = lax.axis_index("cols")
    block = lax.axis_index("rows")
    core = col % 2
    across_x = lax.axis_index("dp") * 2 + col // 2
    place = jnp.stack([block, core, col, block // RING, block % RING, across_x]).astype(jnp.int32)
    rows, own = panel_weight.shape
    panel = hinv_diag.shape[1]
    gathered = lax.all_gather(hinv_off, "rows", axis=0, tiled=True)
    mine = pl.pallas_call(
        factor_kernel,
        in_specs=[SMEM, VMEM],
        out_specs=VMEM,
        out_shape=jax.ShapeDtypeStruct((BLOCK, panel // 8), F32),
        cost_estimate=cost(2 * 64 * 64 * 1600 * 6, 2 * 64 * 1024 * 4),
    )(place, hinv_diag)

    part = lax.all_to_all(jnp.broadcast_to(mine[None], (RING * RING, *mine.shape)), "rows", 0, 0)
    part = part.reshape(panel, panel // 8)
    across = swap(panel_weight, 2)
    dense = forward(place, panel_weight, calib_panel, rest_weight, calib_rest)
    part, across, dense = lax.optimization_barrier((part, across, dense))

    next_x = both_ways(part, "x")
    pieces = [panel_weight, swap(panel_weight, 1), across]
    next_x, pieces = lax.optimization_barrier((next_x, pieces))
    far_x = onward(halves(next_x), "x")
    pieces.append(swap(across, 1))
    near = jnp.stack([part, *next_x, jnp.concatenate(far_x)])
    far = swap(near, 1)

    high, low, kept = pl.pallas_call(
        chain_kernel,
        in_specs=[SMEM, SMEM] + [VMEM] * 6,
        out_specs=[VMEM] * 3,
        out_shape=[jax.ShapeDtypeStruct((rows, panel), BF16)] * 2
        + [jax.ShapeDtypeStruct((rows, own), F32)],
        scratch_shapes=[
            pltpu.VMEM((4, rows, own), F32),
            pltpu.VMEM((panel, panel), BF16),
            pltpu.VMEM((panel, panel), BF16),
            pltpu.VMEM((4, rows, own), F32),
        ],
        compiler_params=params(24),
        cost_estimate=cost(2 * rows * panel * panel * 6, rows * panel * 8 + panel * panel * 4),
    )(place, prune_blocks, *pieces, near, far)
    dense = scatter_sum(*dense)
    gathered, dense = lax.optimization_barrier((gathered, dense))
    new_rest, keep, send = update(
        place, kept, calib_panel, (high, low), rest_weight, gathered, calib_rest
    )
    pruned = scatter_sum(keep, send)
    return kept, new_rest, pruned.astype(BF16), pruned - dense


def solution(mesh):
    in_specs = (
        P("rows", "cols"),
        P("rows", "cols"),
        P("rows", None),
        P("rows", "cols"),
        P("dp", "cols"),
        P("dp", "cols"),
        P("rows", None),
    )
    out_specs = (
        P("rows", "cols"),
        P("rows", "cols"),
        P("dp", ("rows", "cols")),
        P("dp", ("rows", "cols")),
    )
    return jax.shard_map(
        on_device, mesh=mesh, in_specs=in_specs, out_specs=out_specs, check_vma=False
    )
```

```python
import functools

import jax
import jax.numpy as jnp
from jax import lax
from jax.experimental import pallas as pl
from jax.experimental.pallas import tpu as pltpu
from jax.sharding import PartitionSpec as P

BLOCK = 64
UPDATE_MIB = 53
RING = 4
OFFSETS = (0, -1, 1, 2)
GROUP = 256
TILE = 768
F32 = jnp.float32
BF16 = jnp.bfloat16
HIGHEST = lax.Precision.HIGHEST


def split(value):
    high = value.astype(BF16)
    low = (value - high.astype(F32)).astype(BF16)
    return high, low


def dot(left, right):
    return jnp.dot(left, right, preferred_element_type=F32)


def dot3(left, right):
    return dot(left[0], right[0]) + dot(left[1], right[0]) + dot(left[0], right[1])


def dot_nt(left, right):
    return lax.dot_general(left, right, (((1,), (1,)), ((), ())), preferred_element_type=F32)


def along(value, axis, step):
    if axis == "x":
        pairs = []
        for x in range(RING):
            to = (x + step) % RING
            for core in range(2):
                pairs.append((((x % 2) * 2 + core) * 2 + x // 2, ((to % 2) * 2 + core) * 2 + to // 2))
        return lax.ppermute(value, ("cols", "dp"), pairs)

    def shift(y, z):
        if axis == "y":
            return ((y + step) % RING) * RING + z
        return y * RING + (z + step) % RING

    pairs = [(y * RING + z, shift(y, z)) for y in range(RING) for z in range(RING)]
    return lax.ppermute(value, "rows", pairs)


def swap(value, bit):
    return lax.ppermute(value, "cols", [(i, i ^ bit) for i in range(4)])


def both_ways(value, axis):
    return along(value, axis, 1), along(value, axis, -1)


def halves(pair):
    before, after = pair
    half = before.shape[0] // 2
    return before[:half], after[half:]


def onward(pair, axis):
    top, bottom = pair
    return along(top, axis, 1), along(bottom, axis, -1)


def after(value, *others):
    return lax.optimization_barrier((value, others))[0]


def ring_gather(value, axis):
    pair = both_ways(value, axis)
    return jnp.concatenate([value, *pair, *onward(halves(pair), axis)])


def factor_kernel(place, rows_ref, out_ref):
    block, core = place[0], place[1]
    side = BLOCK
    row = lax.broadcasted_iota(jnp.int32, (side, side), 0)
    column = lax.broadcasted_iota(jnp.int32, (side, side), 1)
    pair = rows_ref[:, pl.ds(pl.multiple_of((block >> 1) * 128, 128), 128)]
    square = jnp.where((block & 1) != 0, pair[:, side:], pair[:, :side])
    identity = (row == column).astype(F32)
    down = jnp.sum(square * identity, axis=1, keepdims=True)
    across = jnp.sum(square * identity, axis=0, keepdims=True)
    power = jnp.where(column > row, -(square / down), 0.0)
    inverse = identity + power
    for _ in range(side.bit_length() - 2):
        power = jnp.dot(power, power, precision=HIGHEST, preferred_element_type=F32)
        inverse = jnp.dot(inverse, identity + power, precision=HIGHEST, preferred_element_type=F32)
    inverse = inverse / across
    width = out_ref.shape[1]
    start = pl.multiple_of((place[5] * 2 + core) * width, width)
    mine = rows_ref[:, pl.ds(start, width)]
    local = lax.broadcasted_iota(jnp.int32, (side, width), 1) + start - block * side
    wide_row = lax.broadcasted_iota(jnp.int32, (side, width), 0)
    inside = (local >= 0) & (local < side)
    mine = jnp.where(inside, (local == wide_row).astype(F32), mine)
    out_ref[...] = jnp.dot(inverse, mine, precision=HIGHEST, preferred_element_type=F32)


def chain_kernel(
    place, prune_ref, w0, w1, w2, w3, near_ref, far_ref,
    high_ref, low_ref, kept_ref,
    work, fac_high, fac_low, kept,
):
    col, core, y, z, x = place[2], place[1], place[3], place[4], place[5]
    rows, own = w0.shape
    for slot, piece in enumerate((w0, w1, w2, w3)):
        work[col ^ slot] = piece[...]
    width = near_ref.shape[-1]
    for which, ref in enumerate((near_ref, far_ref)):
        for slot, offset in enumerate(OFFSETS):
            piece = ((x + offset) & 3) * 2 + (core ^ which)
            start = pl.multiple_of(piece * width, width)
            for outer, zo in enumerate(OFFSETS):
                for inner, yo in enumerate(OFFSETS):
                    block = ((y + yo) & 3) * RING + ((z + zo) & 3)
                    top = pl.multiple_of(block * BLOCK, BLOCK)
                    at = (outer * RING + inner) * BLOCK
                    high, low = split(ref[slot, at : at + BLOCK, :])
                    fac_high[pl.ds(top, BLOCK), pl.ds(start, width)] = high
                    fac_low[pl.ds(top, BLOCK), pl.ds(start, width)] = low
    groups = rows // BLOCK
    bits = []
    for group in range(groups):
        word = jnp.int32(0)
        for entry in range(prune_ref.shape[1]):
            word = word | (jnp.int32(1) << prune_ref[group, entry])
        bits.append(jnp.full((BLOCK, 128), word, jnp.int32))
    lane = lax.broadcasted_iota(jnp.int32, (rows, 128), 1)
    upper = lane >> 6
    bits = lax.shift_right_logical(jnp.concatenate(bits, axis=0), upper)
    lower = 1 - upper
    panels = work.shape[0]
    parts = 2
    size = rows // parts
    for panel in range(panels):
        base = panel * own
        for part in range(parts):
            rs = slice(part * size, (part + 1) * size)
            word, first_half = bits[rs], lower[rs]
            left = work[panel, rs, :128]
            right = work[panel, rs, 128:]
            targets = []
            pair_values = [left, right]
            for pair in range(2):
                value = pair_values[pair]
                first = panel * 4 + pair * 2
                top = base + pair * 128
                hit = lax.shift_right_logical(word, first) & 1
                t0 = jnp.where((hit & first_half) != 0, value, 0.0)
                fac = (
                    fac_high[top : top + 128, top : top + 128],
                    fac_low[top : top + 128, top : top + 128],
                )
                step = dot3(split(t0), fac)
                value = jnp.where(first_half != 0, value, value - step)
                target = jnp.where(hit != 0, value, 0.0)
                keep = jnp.where(hit != 0, 0.0, value)
                kept[panel, rs, pair * 128 : (pair + 1) * 128] = keep
                targets.append(target)
                if pair == 0:
                    fac = (
                        fac_high[top : top + 128, top + 128 : top + 256],
                        fac_low[top : top + 128, top + 128 : top + 256],
                    )
                    pair_values[1] = right - dot3(split(target), fac)
            target = split(jnp.concatenate(targets, axis=1))
            r = lax.broadcasted_iota(jnp.int32, (own, own), 0)
            c = lax.broadcasted_iota(jnp.int32, (own, own), 1)
            same = (r // BLOCK) == (c // BLOCK)
            zero = jnp.zeros((own, own), BF16)
            diagonal = (
                jnp.where(same, fac_high[base : base + own, base : base + own], zero),
                jnp.where(same, fac_low[base : base + own, base : base + own], zero),
            )
            errors = split(dot3(target, diagonal))
            high_ref[rs, base : base + own] = errors[0]
            low_ref[rs, base : base + own] = errors[1]
            for later in range(panel + 1, panels):
                to = later * own
                fac = (
                    fac_high[base : base + own, to : to + own],
                    fac_low[base : base + own, to : to + own],
                )
                work[later, rs, :] = work[later, rs, :] - dot3(target, fac)
    kept_ref[...] = kept[col]


def store_slots(place, total, refs):
    col = place[2]
    width = refs[0].shape[1]
    for slot, ref in enumerate(refs):
        group = col ^ slot
        for source in range(4):

            @pl.when(group == source)
            def _():
                ref[...] = total[:, source * width : (source + 1) * width]


def forward_kernel(place, panel_ref, calib_panel_ref, rest_ref, calib_ref, k0, s0, k1, s1, total):
    step = pl.program_id(0)

    @pl.when(step == 0)
    def _():
        total[...] = dot_nt(calib_panel_ref[...], panel_ref[...].astype(BF16))

    total[...] += dot_nt(calib_ref[...], rest_ref[...].astype(BF16))

    @pl.when(step == pl.num_programs(0) - 1)
    def _():
        store_slots(place, total, (k0, s0, k1, s1))


def update_kernel(
    place, panel_ref, calib_panel_ref, high_ref, low_ref, rest_ref, factor_ref, calib_ref,
    new_ref, k0, s0, k1, s1, total,
):
    step = pl.program_id(0)

    @pl.when(step == 0)
    def _():
        total[...] = dot_nt(calib_panel_ref[...], panel_ref[...].astype(BF16))

    value = rest_ref[...] - dot3((high_ref[...], low_ref[...]), split(factor_ref[...]))
    new_ref[...] = value
    total[...] += dot_nt(calib_ref[...], value.astype(BF16))

    @pl.when(step == pl.num_programs(0) - 1)
    def _():
        store_slots(place, total, (k0, s0, k1, s1))


SMEM = pl.BlockSpec(memory_space=pltpu.SMEM)
VMEM = pl.BlockSpec(memory_space=pltpu.VMEM)


def params(mib, **more):
    return pltpu.CompilerParams(vmem_limit_bytes=mib * 2**20, **more)


def cost(flops, moved):
    return pl.CostEstimate(flops=flops, bytes_accessed=moved, transcendentals=0)


def slots(rows, tokens):
    shape = jax.ShapeDtypeStruct((tokens, rows // 4), F32)
    return [shape] * 4, [whole(shape.shape)] * 4


def whole(shape):
    return pl.BlockSpec(shape, lambda i: (0,) * len(shape))


def tiles(rows, width):
    return pl.BlockSpec((rows, width), lambda i: (0, i))


def forward(place, panel, calib_panel, rest, calib):
    rows, columns = rest.shape
    tokens = calib.shape[0]
    tile = 384
    shapes, specs = slots(rows, tokens)
    return pl.pallas_call(
        forward_kernel,
        grid=(columns // tile,),
        in_specs=[
            SMEM, whole(panel.shape), whole(calib_panel.shape),
            tiles(rows, tile), tiles(tokens, tile),
        ],
        out_specs=specs,
        out_shape=shapes,
        scratch_shapes=[pltpu.VMEM((tokens, rows), F32)],
        compiler_params=params(16),
        cost_estimate=cost(2 * rows * tokens * columns, rows * columns * 4 + tokens * columns * 2),
    )(place, panel, calib_panel, rest, calib)


def update(place, panel, calib_panel, errors, rest, factor, calib):
    rows, columns = rest.shape
    tokens = calib.shape[0]
    depth = factor.shape[0]
    shapes, specs = slots(rows, tokens)
    operands = (place, panel, calib_panel, *errors, rest, factor, calib)
    return pl.pallas_call(
        update_kernel,
        grid=(columns // TILE,),
        in_specs=[SMEM] + [whole(v.shape) for v in operands[1:5]]
        + [tiles(rows, TILE), tiles(depth, TILE), tiles(tokens, TILE)],
        out_specs=[tiles(rows, TILE)] + specs,
        out_shape=[jax.ShapeDtypeStruct(rest.shape, F32)] + shapes,
        scratch_shapes=[pltpu.VMEM((tokens, rows), F32)],
        compiler_params=params(UPDATE_MIB),
        cost_estimate=cost(
            2 * rows * columns * (3 * depth + tokens), columns * 4 * (2 * rows + depth)
        ),
    )(*operands)


def scatter_sum(k0, s0, k1, s1):
    ahead = swap(s1, 1)
    stays = swap(s0, 1)
    return k0 + stays + swap(k1 + ahead, 2)


def on_device(
    panel_weight, rest_weight, hinv_diag, hinv_off, calib_panel, calib_rest, prune_blocks
):
    col = lax.axis_index("cols")
    block = lax.axis_index("rows")
    core = col % 2
    across_x = lax.axis_index("dp") * 2 + col // 2
    place = jnp.stack([block, core, col, block // RING, block % RING, across_x]).astype(jnp.int32)
    rows, own = panel_weight.shape
    panel = hinv_diag.shape[1]
    gathered = lax.all_gather(hinv_off, "rows", axis=0, tiled=True)
    mine = pl.pallas_call(
        factor_kernel,
        in_specs=[SMEM, VMEM],
        out_specs=VMEM,
        out_shape=jax.ShapeDtypeStruct((BLOCK, panel // 8), F32),
        cost_estimate=cost(2 * 64 * 64 * 1600 * 6, 2 * 64 * 1024 * 4),
    )(place, hinv_diag)

    part = ring_gather(ring_gather(mine, "y"), "z")
    across = swap(panel_weight, 2)
    dense = forward(place, panel_weight, calib_panel, rest_weight, calib_rest)
    part, across, dense = lax.optimization_barrier((part, across, dense))

    next_x = both_ways(part, "x")
    pieces = [panel_weight, swap(panel_weight, 1), across]
    next_x, pieces = lax.optimization_barrier((next_x, pieces))
    far_x = onward(halves(next_x), "x")
    pieces.append(swap(across, 1))
    near = jnp.stack([part, *next_x, jnp.concatenate(far_x)])
    far = swap(near, 1)

    high, low, kept = pl.pallas_call(
        chain_kernel,
        in_specs=[SMEM, SMEM] + [VMEM] * 6,
        out_specs=[VMEM] * 3,
        out_shape=[jax.ShapeDtypeStruct((rows, panel), BF16)] * 2
        + [jax.ShapeDtypeStruct((rows, own), F32)],
        scratch_shapes=[
            pltpu.VMEM((4, rows, own), F32),
            pltpu.VMEM((panel, panel), BF16),
            pltpu.VMEM((panel, panel), BF16),
            pltpu.VMEM((4, rows, own), F32),
        ],
        compiler_params=params(24),
        cost_estimate=cost(2 * rows * panel * panel * 6, rows * panel * 8 + panel * panel * 4),
    )(place, prune_blocks, *pieces, near, far)
    dense = scatter_sum(*dense)
    gathered, dense = lax.optimization_barrier((gathered, dense))
    new_rest, *parts = update(
        place, kept, calib_panel, (high, low), rest_weight, gathered, calib_rest
    )
    pruned = scatter_sum(*parts)
    return kept, new_rest, pruned.astype(BF16), pruned - dense


def solution(mesh):
    in_specs = (
        P("rows", "cols"),
        P("rows", "cols"),
        P("rows", None),
        P("rows", "cols"),
        P("dp", "cols"),
        P("dp", "cols"),
        P("rows", None),
    )
    out_specs = (
        P("rows", "cols"),
        P("rows", "cols"),
        P("dp", ("rows", "cols")),
        P("dp", ("rows", "cols")),
    )
    return jax.shard_map(
        on_device, mesh=mesh, in_specs=in_specs, out_specs=out_specs, check_vma=False
    )
```
